256 devices in a mesh: slab: 4 (over x), row: 32 (over z, y), col: 2 (over core).
Axes of the slice: x: 4, y: 4, z: 8, core: 2. Of those that a mesh axis runs over, the one named last changes fastest.
Arguments:
- diagonals: bfloat16 [4, 1024, 1024], P('slab', 'row', 'col'), as said below
- lower_neighbour_coupling: bfloat16 [4, 1024, 1024], P('slab', 'row', 'col'), as said below
- upper_neighbour_coupling: bfloat16 [4, 1024, 1024], P('slab', 'row', 'col'), as said below
- right_hand_columns: bfloat16 [4, 1024, 512], P('slab', 'row', 'col'), may hold values from -6 to 6
Outputs:
- diag_out: bfloat16 [4, 1024, 1024], P('slab', 'row', 'col')
- lower_out: bfloat16 [4, 1024, 1024], P('slab', 'row', 'col')
- upper_out: bfloat16 [4, 1024, 1024], P('slab', 'row', 'col')
- sides_out: bfloat16 [4, 1024, 512], P('slab', 'row', 'col')
The draws below stay inside these ranges and needn't reach their ends.
Inputs may be any that keep to these rules, and one draw needn't show every extreme that they name: Each slab's diagonal block has its diagonal in 1 to 2 and small independent entries off it, so that the pivots of all levels are dominated by their diagonals. `lower_neighbour_coupling`: independent entries of magnitude near 0.2 / sqrt(1024). `upper_neighbour_coupling`: independent entries of magnitude near 0.2 / sqrt(1024).
All inputs are finite; a program needn't handle non-finite values.
Results may differ from the reference program's by a relative error of at most 0.0075.
Values may be sent and summed in bfloat16 or wider, within the bound.
A program may use at most 64 MiB of HBM per device.

```python
import math
import jax
import jax.numpy as jnp
from jax import lax

BLOCK = 1024
COLUMNS = 512
SWEEPS = 2
SLAB_TOTAL = 4
LEVELS = 1


def coupling_draw(key):
    noise = jnp.clip(jax.random.normal(key, (SLAB_TOTAL, BLOCK, BLOCK), jnp.float32), -4.0, 4.0)
    return (noise * (0.2 / math.sqrt(BLOCK))).astype(jnp.bfloat16)


def draw_diagonals(key, part):
    noise_key, center_key = jax.random.split(jax.random.fold_in(key, 13))
    noise = jnp.clip(jax.random.normal(noise_key, (SLAB_TOTAL, BLOCK, BLOCK), jnp.float32), -4.0, 4.0)
    offdiag = noise * (0.3 / math.sqrt(BLOCK))
    center = jax.random.uniform(center_key, (SLAB_TOTAL, BLOCK), jnp.float32, 1.0, 2.0)
    eye_mask = jnp.eye(BLOCK, dtype=jnp.float32)
    return (offdiag * (1.0 - eye_mask) + eye_mask * center[:, :, None]).astype(jnp.bfloat16)


def draw_lower_neighbour_coupling(key, part):
    return coupling_draw(jax.random.fold_in(key, 11))


def draw_upper_neighbour_coupling(key, part):
    return coupling_draw(jax.random.fold_in(key, 12))


def block_levels(stream_key, shape, cuts, least, top_value):
    level = 1.0
    for axis_at, parts in cuts:
        draws = jax.random.uniform(jax.random.fold_in(jax.random.fold_in(stream_key, 6), axis_at), (parts,), jnp.float32, least / len(cuts), top_value / len(cuts))
        level = level * jnp.repeat(jnp.exp(draws), shape[axis_at] // parts).reshape((-1,) + (1,) * (len(shape) - 1 - axis_at))
    return level


def normal_values(stream_key, shape, scale, reach, pieces=(), held_as=jnp.bfloat16):
    values = scale * jax.random.normal(stream_key, shape, jnp.float32)
    if pieces:
        values = values * block_levels(stream_key, shape, pieces, -0.22, 0.18)
    return jnp.clip(values, -reach, reach).astype(held_as)


def setup_inputs(seed: int = 0) -> dict:
    streams_of = jax.random.split(jax.random.key(seed), 5)
    diagonals = draw_diagonals(jax.random.fold_in(streams_of[4], 71), 0)
    lower_neighbour_coupling = draw_lower_neighbour_coupling(jax.random.fold_in(streams_of[4], 71), 0)
    upper_neighbour_coupling = draw_upper_neighbour_coupling(jax.random.fold_in(streams_of[4], 71), 0)
    right_hand_columns = normal_values(streams_of[3], (SLAB_TOTAL, BLOCK, COLUMNS), 1.0, 6.0, ((0, 4), (1, 32), (2, 2)))
    return {"diagonals": diagonals, "lower_neighbour_coupling": lower_neighbour_coupling, "upper_neighbour_coupling": upper_neighbour_coupling, "right_hand_columns": right_hand_columns}


def jacobi_multiplier(stacked_blocks, pivot_block):
    pivot_full = pivot_block.astype(jnp.float32)
    divisor = jnp.diagonal(pivot_full)
    target = stacked_blocks.astype(jnp.float32)
    iterate = (target / divisor).astype(jnp.bfloat16)
    for sweep_index in range(SWEEPS):
        product = jnp.einsum("akm,mn->akn", iterate.astype(jnp.float32), pivot_full, precision=lax.Precision.HIGHEST)
        iterate = (iterate.astype(jnp.float32) + (target - product) / divisor).astype(jnp.bfloat16)
    return iterate


def reference(diagonals, lower_neighbour_coupling, upper_neighbour_coupling, right_hand_columns):
    zeros_block = jnp.zeros((BLOCK, BLOCK), jnp.bfloat16)
    zeros_wide = jnp.zeros((BLOCK, 2 * BLOCK + COLUMNS), jnp.bfloat16)
    lower_neighbour_coupling = lower_neighbour_coupling.at[0].set(zeros_block)
    upper_neighbour_coupling = upper_neighbour_coupling.at[SLAB_TOTAL - 1].set(zeros_block)
    for level_index in range(LEVELS):
        level_stride = 2 ** level_index
        toward_right = {}
        toward_left = {}
        for eliminate_level in range(SLAB_TOTAL):
            if eliminate_level - level_stride >= 0:
                left_upper_block = upper_neighbour_coupling[eliminate_level - level_stride]
            else:
                left_upper_block = zeros_block
            if eliminate_level + level_stride < SLAB_TOTAL:
                right_lower_block = lower_neighbour_coupling[eliminate_level + level_stride]
            else:
                right_lower_block = zeros_block
            stacked_blocks = jnp.stack([right_lower_block, left_upper_block])
            scaling_factor = jacobi_multiplier(stacked_blocks, diagonals[eliminate_level])
            hand_sides = jnp.concatenate([upper_neighbour_coupling[eliminate_level], lower_neighbour_coupling[eliminate_level], right_hand_columns[eliminate_level]], axis=1).astype(jnp.float32)
            block_products = jnp.einsum("akm,mn->akn", scaling_factor.astype(jnp.float32), hand_sides, precision=lax.Precision.HIGHEST).astype(jnp.bfloat16)
            if eliminate_level + level_stride < SLAB_TOTAL:
                toward_right[eliminate_level + level_stride] = block_products[0]
            if eliminate_level - level_stride >= 0:
                toward_left[eliminate_level - level_stride] = block_products[1]
        new_diag = []
        new_lower = []
        new_upper = []
        new_sides = []
        for keep in range(SLAB_TOTAL):
            from_left = toward_right[keep] if keep in toward_right else zeros_wide
            from_right = toward_left[keep] if keep in toward_left else zeros_wide
            reduced_pivot = diagonals[keep].astype(jnp.float32) - from_left[:, :BLOCK].astype(jnp.float32) - from_right[:, BLOCK:2 * BLOCK].astype(jnp.float32)
            reduced_sides = right_hand_columns[keep].astype(jnp.float32) - from_left[:, 2 * BLOCK:].astype(jnp.float32) - from_right[:, 2 * BLOCK:].astype(jnp.float32)
            new_diag.append(reduced_pivot.astype(jnp.bfloat16))
            new_sides.append(reduced_sides.astype(jnp.bfloat16))
            new_lower.append(-from_left[:, BLOCK:2 * BLOCK])
            new_upper.append(-from_right[:, :BLOCK])
        diagonals = jnp.stack(new_diag)
        right_hand_columns = jnp.stack(new_sides)
        lower_neighbour_coupling = jnp.stack(new_lower)
        upper_neighbour_coupling = jnp.stack(new_upper)
    return diagonals, lower_neighbour_coupling, upper_neighbour_coupling, right_hand_columns
```

```python
import functools

import jax
import jax.numpy as jnp
from jax import lax
from jax.experimental import pallas as pl
from jax.experimental.pallas import tpu as pltpu
from jax.sharding import PartitionSpec as P

MESH = pl.DeviceIdType.MESH
SWEEPS = 2
SLABS, ZS, YS, CORES = 4, 8, 4, 2
ROWS = 32
HALF = 512
TILE = 128
BAND = YS * ROWS
PACKED = BAND + ROWS
NEAR_FIRST = (1, 7, 2, 6, 3, 5, 4)
FAR_FIRST = (4, 3, 5, 2, 6, 1, 7)


def kernel(
    pivot_in, lower_in, upper_in, sides_in,
    pivot_out, lower_out, upper_out, sides_out,
    pivot_own, lower_own, upper_own, sides_own,
    pivot, stacked, sides_raw, hand, sides_full, iterate, product, update,
    load_sem, z_send, z_recv, y_send, y_recv, core_send, core_recv,
    stack_send, stack_recv, pass_send, pass_recv, deal_send, deal_recv,
    ring_send, ring_recv, back_send, back_recv,
):
    x = lax.axis_index("slab")
    row = lax.axis_index("row")
    z, y = row // YS, row % YS
    c = lax.axis_index("col")

    def at(dx=0, dz=0, dy=0, dc=0):
        there = lax.rem(z + dz, ZS) * YS + lax.rem(y + dy, YS)
        return (lax.rem(x + dx, SLABS), there, lax.rem(c + dc, CORES))

    def remote(src, dst, send, recv, where):
        return pltpu.make_async_remote_copy(
            src_ref=src, dst_ref=dst, send_sem=send, recv_sem=recv,
            device_id=where, device_id_type=MESH,
        )

    def lanes(block, width=TILE):
        return pl.ds(pl.multiple_of(block * width, TILE), width)

    def band_rows(piece):
        return pl.ds(pl.multiple_of(piece * ROWS, ROWS), ROWS)

    loads = [
        pltpu.make_async_copy(pivot_in, pivot.at[c, z, y], load_sem.at[0]),
        pltpu.make_async_copy(upper_in, upper_own, load_sem.at[1]),
        pltpu.make_async_copy(lower_in, lower_own, load_sem.at[2]),
        pltpu.make_async_copy(sides_in, sides_own, load_sem.at[3]),
        pltpu.make_async_copy(upper_in.at[:, lanes(y)], hand.at[z, band_rows(y), pl.ds(0, TILE)], load_sem.at[4]),
        pltpu.make_async_copy(lower_in.at[:, lanes(y)], hand.at[z, band_rows(y), pl.ds(TILE, TILE)], load_sem.at[5]),
        pltpu.make_async_copy(sides_in.at[:, lanes(y // 2)], sides_raw.at[y], load_sem.at[6]),
        pltpu.make_async_copy(pivot_in, pivot_own, load_sem.at[7]),
    ]
    for load in loads:
        load.start()
    partners = [at(dz=d) for d in range(1, ZS)] + [at(dy=d) for d in range(1, YS)] + [at(dc=1)]
    partners += [at(dx=dx, dy=dy) for dx in (1, 3) for dy in range(YS)]
    barrier = pltpu.get_barrier_semaphore()
    for partner in partners:
        pl.semaphore_signal(barrier, inc=1, device_id=partner, device_id_type=MESH)
    for load in loads:
        load.wait()
    pl.semaphore_wait(barrier, len(partners))

    def z_copy(d):
        mine = pivot.at[c, z, y]
        return remote(mine, mine, z_send.at[d], z_recv.at[d], at(dz=d))

    def y_copy(d, dy):
        zs = lax.rem(z + ZS - d, ZS)
        mine = pivot.at[c, zs, y]
        return remote(mine, mine, y_send.at[d, dy], y_recv.at[d, dy], at(dy=dy))

    def core_copy(d, dy):
        zs, ys = lax.rem(z + ZS - d, ZS), lax.rem(y + YS - dy, YS)
        mine = pivot.at[c, zs, ys]
        return remote(mine, mine, core_send, core_recv, at(dc=1))

    def deal_copies(dy):
        to = lax.rem(y + dy, YS)
        rows = band_rows(y)
        where = at(dy=dy)
        return [
            remote(upper_own.at[:, lanes(to)], hand.at[z, rows, pl.ds(0, TILE)], deal_send.at[dy, 0], deal_recv.at[dy, 0], where),
            remote(lower_own.at[:, lanes(to)], hand.at[z, rows, pl.ds(TILE, TILE)], deal_send.at[dy, 1], deal_recv.at[dy, 1], where),
            remote(sides_own.at[:, lanes(to // 2)], sides_raw.at[y], deal_send.at[dy, 2], deal_recv.at[dy, 2], where),
        ]

    def stack_copies(dy):
        return [
            remote(lower_own, stacked.at[0, c, y], stack_send.at[0, dy], stack_recv.at[0, dy], at(dx=3, dy=dy)),
            remote(upper_own, stacked.at[1, c, y], stack_send.at[1, dy], stack_recv.at[1, dy], at(dx=1, dy=dy)),
        ]

    def pass_copies():
        return [
            remote(stacked.at[a, c], stacked.at[a, c], pass_send.at[a], pass_recv.at[a], at(dc=1))
            for a in range(2)
        ]

    def ring_copy(way, step, part):
        zs = lax.rem(z + (ZS - step if way == 0 else step), ZS)
        rows = hand.at[zs, pl.ds(part * (PACKED // 2), PACKED // 2)]
        return remote(rows, rows, ring_send.at[way, step, part], ring_recv.at[way, step, part], at(dz=1 if way == 0 else ZS - 1))

    def ring_parts(way, step):
        return (0, 1) if step < 3 else (way,)

    for d in FAR_FIRST:
        z_copy(d).start()
    for dy in (2, 1, 3):
        for copy in deal_copies(dy):
            copy.start()
    core_copy(0, 0).start()
    for dy in (2, 1, 3):
        y_copy(0, dy).start()
    for dy in range(YS):
        for copy in stack_copies(dy):
            copy.start()

    lane = lax.broadcasted_iota(jnp.int32, (ROWS, TILE), 1)
    left = lane < TILE // 2
    odd = lax.rem(y, 2) == 1

    for dy in range(1, YS):
        for copy in deal_copies(dy):
            copy.wait_recv()
    for t in range(2):
        low = sides_raw[2 * t].astype(jnp.float32)
        high = sides_raw[2 * t + 1].astype(jnp.float32)
        low = jnp.where(odd, pltpu.roll(low, TILE // 2, 1), low)
        high = jnp.where(odd, high, pltpu.roll(high, TILE // 2, 1))
        hand[z, BAND:PACKED, t * TILE:(t + 1) * TILE] = jnp.where(left, low, high).astype(jnp.bfloat16)

    def ring_start(step):
        for part in range(2):
            for way in range(2):
                if part in ring_parts(way, step):
                    ring_copy(way, step, part).start()

    def ring_wait(step):
        for part in range(2):
            for way in range(2):
                if part in ring_parts(way, step):
                    ring_copy(way, step, part).wait_recv()

    def ring_on(step):
        for part in range(2):
            for way in range(2):
                if part in ring_parts(way, step):
                    ring_copy(way, step, part).wait_recv()
                if step < 3 and part in ring_parts(way, step + 1):
                    ring_copy(way, step + 1, part).start()

    def z_arrival(d):
        z_copy(d).wait_recv()
        for dy in (2, 1, 3):
            y_copy(d, dy).start()
        core_copy(d, 0).start()

    def y_arrival(d):
        for dy in (1, 3, 2):
            y_copy(d, dy).wait_recv()
            core_copy(d, dy).start()

    ring_start(0)
    for d in (1, 7, 2, 6):
        z_arrival(d)
    ring_on(0)
    y_arrival(0)
    for d in (3, 5, 4):
        z_arrival(d)
    y_arrival(1)
    y_arrival(7)
    ring_on(1)
    for dy in range(YS):
        for copy in stack_copies(dy):
            copy.wait_recv()
    for copy in pass_copies():
        copy.start()
    y_arrival(2)
    y_arrival(6)
    ring_on(2)
    for d in (3, 5, 4):
        y_arrival(d)

    for copy in pass_copies():
        copy.wait_recv()
    theirs = pivot.at[1 - c]
    remote(theirs, theirs, core_send, core_recv, at(dc=1)).wait_recv()

    eye = lax.broadcasted_iota(jnp.int32, (BAND, TILE), 0) == lax.broadcasted_iota(jnp.int32, (BAND, TILE), 1)

    def inverse_of(h):
        found = []
        for t in range(HALF // TILE):
            block = pivot[h, h * (ZS // 2) + t, :, :, t * TILE:(t + 1) * TILE].reshape(BAND, TILE)
            found.append(jnp.sum(jnp.where(eye, block.astype(jnp.float32), 0.0), axis=0, keepdims=True))
        return 1.0 / jnp.concatenate(found, axis=1)

    inverse = [inverse_of(h) for h in range(CORES)]
    present = [x < SLABS - 1, x > 0]

    def target(a, h):
        block = stacked[a, h].reshape(BAND, HALF).astype(jnp.float32)
        return jnp.where(present[a], block, 0.0)

    for a in range(2):
        for h in range(CORES):
            iterate[0, a * BAND:(a + 1) * BAND, h * HALF:(h + 1) * HALF] = (target(a, h) * inverse[h]).astype(jnp.bfloat16)
    for sweep in range(SWEEPS):
        now, later = sweep % 2, (sweep + 1) % 2
        for h in range(CORES):
            columns = slice(h * HALF, (h + 1) * HALF)
            product[...] = jnp.dot(iterate[now], pivot[h].reshape(ZS * BAND, HALF), preferred_element_type=jnp.float32)
            for a in range(2):
                rows = slice(a * BAND, (a + 1) * BAND)
                step = (target(a, h) - product[rows]) * inverse[h]
                iterate[later, rows, columns] = (iterate[now, rows, columns].astype(jnp.float32) + step).astype(jnp.bfloat16)

    ring_wait(3)
    for zs in range(ZS):
        for t in range(2):
            packed = hand[zs, BAND:PACKED, t * TILE:(t + 1) * TILE].astype(jnp.float32)
            turned = pltpu.roll(packed, TILE // 2, 1)
            sides_full[zs, 2 * t] = jnp.where(odd, turned, packed).astype(jnp.bfloat16)
            sides_full[zs, 2 * t + 1] = jnp.where(odd, packed, turned).astype(jnp.bfloat16)
    factor = iterate[SWEEPS % 2]
    coupled = jnp.dot(factor, hand[:, :BAND, :].reshape(ZS * BAND, 2 * TILE), preferred_element_type=jnp.float32)
    upper_part = jnp.where(present[0], coupled[:, :TILE], 0.0).astype(jnp.bfloat16)
    lower_part = jnp.where(present[1], coupled[:, TILE:], 0.0).astype(jnp.bfloat16)
    product[:, :TILE] = jnp.dot(factor, sides_full[...].reshape(ZS * BAND, TILE), preferred_element_type=jnp.float32)
    sides_part = product[:, :TILE].astype(jnp.bfloat16)
    for a in range(2):
        rows = slice(a * BAND, (a + 1) * BAND)
        update[0, a, :, :, 0:TILE] = upper_part[rows].reshape(YS, ROWS, TILE)
        update[0, a, :, :, TILE:2 * TILE] = lower_part[rows].reshape(YS, ROWS, TILE)
        update[0, a, :, :, 2 * TILE:] = sides_part[rows].reshape(YS, ROWS, TILE)

    def back_copy(a, dy):
        to = lax.rem(y + dy, YS)
        return remote(update.at[0, a, to], update.at[1, a, y], back_send.at[a, dy], back_recv.at[a, dy], at(dx=1 if a == 0 else 3, dy=dy))

    for dy in (2, 1, 3, 0):
        for a in range(2):
            back_copy(a, dy).start()
    for dy in range(YS):
        for a in range(2):
            back_copy(a, dy).wait_recv()

    for t in range(YS):
        columns = slice(t * TILE, (t + 1) * TILE)
        before, after = update[1, 0, t].astype(jnp.float32), update[1, 1, t].astype(jnp.float32)
        reduced = pivot_own[:, columns].astype(jnp.float32) - before[:, :TILE] - after[:, TILE:2 * TILE]
        pivot_out[:, columns] = reduced.astype(jnp.bfloat16)
        lower_out[:, columns] = (-before[:, TILE:2 * TILE]).astype(jnp.bfloat16)
        upper_out[:, columns] = (-after[:, :TILE]).astype(jnp.bfloat16)
    for t in range(2):
        columns = slice(t * TILE, (t + 1) * TILE)
        terms = [
            jnp.where(left, update[1, a, 2 * t, :, 2 * TILE:].astype(jnp.float32), update[1, a, 2 * t + 1, :, 2 * TILE:].astype(jnp.float32))
            for a in range(2)
        ]
        reduced = sides_own[:, columns].astype(jnp.float32) - terms[0] - terms[1]
        sides_out[:, columns] = reduced.astype(jnp.bfloat16)

    for d in FAR_FIRST:
        z_copy(d).wait_send()
    for dy in range(1, YS):
        for copy in deal_copies(dy):
            copy.wait_send()
        for d in range(ZS):
            y_copy(d, dy).wait_send()
    for dy in range(YS):
        for copy in stack_copies(dy):
            copy.wait_send()
        for a in range(2):
            back_copy(a, dy).wait_send()
    for copy in pass_copies():
        copy.wait_send()
    mine = pivot.at[c]
    remote(mine, mine, core_send, core_recv, at(dc=1)).wait_send()
    for step in range(4):
        for way in range(2):
            for part in ring_parts(way, step):
                ring_copy(way, step, part).wait_send()


def per_device(diagonals, lower, upper, sides):
    square = jax.ShapeDtypeStruct((ROWS, HALF), jnp.bfloat16)
    wide = jax.ShapeDtypeStruct((ROWS, HALF // 2), jnp.bfloat16)
    whole = pl.BlockSpec(memory_space=pltpu.VMEM)
    bf16 = jnp.bfloat16
    dma = pltpu.SemaphoreType.DMA
    outs = pl.pallas_call(
        kernel,
        out_shape=(square, square, square, wide),
        in_specs=[pl.BlockSpec(memory_space=pl.ANY)] * 4,
        out_specs=(whole,) * 4,
        scratch_shapes=[
            pltpu.VMEM((ROWS, HALF), bf16),
            pltpu.VMEM((ROWS, HALF), bf16),
            pltpu.VMEM((ROWS, HALF), bf16),
            pltpu.VMEM((ROWS, HALF // 2), bf16),
            pltpu.VMEM((CORES, ZS, YS, ROWS, HALF), bf16),
            pltpu.VMEM((2, CORES, YS, ROWS, HALF), bf16),
            pltpu.VMEM((YS, ROWS, TILE), bf16),
            pltpu.VMEM((ZS, PACKED, 2 * TILE), bf16),
            pltpu.VMEM((ZS, YS, ROWS, TILE), bf16),
            pltpu.VMEM((2, 2 * BAND, CORES * HALF), bf16),
            pltpu.VMEM((2 * BAND, HALF), jnp.float32),
            pltpu.VMEM((2, 2, YS, ROWS, 3 * TILE), bf16),
            dma((8,)),
            dma((ZS,)), dma((ZS,)),
            dma((ZS, YS)), dma((ZS, YS)),
            dma, dma,
            dma((2, YS)), dma((2, YS)),
            dma((2,)), dma((2,)),
            dma((YS, 3)), dma((YS, 3)),
            dma((2, 4, 2)), dma((2, 4, 2)),
            dma((2, YS)), dma((2, YS)),
        ],
        compiler_params=pltpu.CompilerParams(
            collective_id=0, has_side_effects=True, vmem_limit_bytes=32 * 2**20
        ),
    )(diagonals[0], lower[0], upper[0], sides[0])
    return tuple(out[None] for out in outs)


def solution(mesh):
    spec = P("slab", "row", "col")
    return jax.shard_map(
        per_device, mesh=mesh, in_specs=(spec,) * 4, out_specs=(spec,) * 4, check_vma=False
    )
```

```python
import functools

import jax
import jax.numpy as jnp
from jax import lax
from jax.experimental import pallas as pl
from jax.experimental.pallas import tpu as pltpu
from jax.sharding import PartitionSpec as P

MESH = pl.DeviceIdType.MESH
SWEEPS = 2
SLABS, ZS, YS, CORES = 4, 8, 4, 2
ROWS = 32
HALF = 512
TILE = 128
BAND = YS * ROWS
PACKED = BAND + ROWS
NEAR_FIRST = (1, 7, 2, 6, 3, 5, 4)


def kernel(
    pivot_in, lower_in, upper_in, sides_in,
    pivot_out, lower_out, upper_out, sides_out,
    pivot_own, lower_own, upper_own, sides_own,
    pivot, stacked, sides_raw, hand, sides_full, iterate, product, update,
    load_sem, z_send, z_recv, y_send, y_recv, core_send, core_recv,
    stack_send, stack_recv, pass_send, pass_recv, deal_send, deal_recv,
    ring_send, ring_recv, back_send, back_recv,
):
    x = lax.axis_index("slab")
    row = lax.axis_index("row")
    z, y = row // YS, row % YS
    c = lax.axis_index("col")

    def at(dx=0, dz=0, dy=0, dc=0):
        there = lax.rem(z + dz, ZS) * YS + lax.rem(y + dy, YS)
        return (lax.rem(x + dx, SLABS), there, lax.rem(c + dc, CORES))

    def remote(src, dst, send, recv, where):
        return pltpu.make_async_remote_copy(
            src_ref=src, dst_ref=dst, send_sem=send, recv_sem=recv,
            device_id=where, device_id_type=MESH,
        )

    def lanes(block, width=TILE):
        return pl.ds(pl.multiple_of(block * width, TILE), width)

    def band_rows(piece):
        return pl.ds(pl.multiple_of(piece * ROWS, ROWS), ROWS)

    loads = [
        pltpu.make_async_copy(pivot_in, pivot.at[c, z, y], load_sem.at[0]),
        pltpu.make_async_copy(upper_in, upper_own, load_sem.at[1]),
        pltpu.make_async_copy(lower_in, lower_own, load_sem.at[2]),
        pltpu.make_async_copy(sides_in, sides_own, load_sem.at[3]),
        pltpu.make_async_copy(upper_in.at[:, lanes(y)], hand.at[z, band_rows(y), pl.ds(0, TILE)], load_sem.at[4]),
        pltpu.make_async_copy(lower_in.at[:, lanes(y)], hand.at[z, band_rows(y), pl.ds(TILE, TILE)], load_sem.at[5]),
        pltpu.make_async_copy(sides_in.at[:, lanes(y // 2)], sides_raw.at[y], load_sem.at[6]),
        pltpu.make_async_copy(pivot_in, pivot_own, load_sem.at[7]),
    ]
    for load in loads:
        load.start()
    partners = [at(dz=d) for d in range(1, ZS)] + [at(dy=d) for d in range(1, YS)] + [at(dc=1)]
    partners += [at(dx=dx, dy=dy) for dx in (1, 3) for dy in range(YS)]
    barrier = pltpu.get_barrier_semaphore()
    for partner in partners:
        pl.semaphore_signal(barrier, inc=1, device_id=partner, device_id_type=MESH)
    for load in loads:
        load.wait()
    pl.semaphore_wait(barrier, len(partners))

    def z_copy(d):
        mine = pivot.at[c, z, y]
        return remote(mine, mine, z_send.at[d], z_recv.at[d], at(dz=d))

    def y_copy(d, dy):
        zs = lax.rem(z + ZS - d, ZS)
        mine = pivot.at[c, zs, y]
        return remote(mine, mine, y_send.at[d, dy], y_recv.at[d, dy], at(dy=dy))

    def core_copy(d, dy):
        zs, ys = lax.rem(z + ZS - d, ZS), lax.rem(y + YS - dy, YS)
        mine = pivot.at[c, zs, ys]
        return remote(mine, mine, core_send, core_recv, at(dc=1))

    def deal_copies(dy):
        to = lax.rem(y + dy, YS)
        rows = band_rows(y)
        where = at(dy=dy)
        return [
            remote(upper_own.at[:, lanes(to)], hand.at[z, rows, pl.ds(0, TILE)], deal_send.at[dy, 0], deal_recv.at[dy, 0], where),
            remote(lower_own.at[:, lanes(to)], hand.at[z, rows, pl.ds(TILE, TILE)], deal_send.at[dy, 1], deal_recv.at[dy, 1], where),
            remote(sides_own.at[:, lanes(to // 2)], sides_raw.at[y], deal_send.at[dy, 2], deal_recv.at[dy, 2], where),
        ]

    def stack_copies(dy):
        return [
            remote(lower_own, stacked.at[0, c, y], stack_send.at[0, dy], stack_recv.at[0, dy], at(dx=3, dy=dy)),
            remote(upper_own, stacked.at[1, c, y], stack_send.at[1, dy], stack_recv.at[1, dy], at(dx=1, dy=dy)),
        ]

    def pass_copies():
        return [
            remote(stacked.at[a, c], stacked.at[a, c], pass_send.at[a], pass_recv.at[a], at(dc=1))
            for a in range(2)
        ]

    def ring_copy(way, step, part):
        zs = lax.rem(z + (ZS - step if way == 0 else step), ZS)
        rows = hand.at[zs, pl.ds(part * (PACKED // 2), PACKED // 2)]
        return remote(rows, rows, ring_send.at[way, step, part], ring_recv.at[way, step, part], at(dz=1 if way == 0 else ZS - 1))

    def ring_parts(way, step):
        return (0, 1) if step < 3 else (way,)

    for d in NEAR_FIRST:
        z_copy(d).start()
    for dy in (2, 1, 3):
        for copy in deal_copies(dy):
            copy.start()
    core_copy(0, 0).start()
    for dy in (2, 1, 3):
        y_copy(0, dy).start()
    for dy in range(YS):
        for copy in stack_copies(dy):
            copy.start()

    lane = lax.broadcasted_iota(jnp.int32, (ROWS, TILE), 1)
    left = lane < TILE // 2
    odd = lax.rem(y, 2) == 1

    for dy in range(1, YS):
        for copy in deal_copies(dy):
            copy.wait_recv()
    for t in range(2):
        low = sides_raw[2 * t].astype(jnp.float32)
        high = sides_raw[2 * t + 1].astype(jnp.float32)
        low = jnp.where(odd, pltpu.roll(low, TILE // 2, 1), low)
        high = jnp.where(odd, high, pltpu.roll(high, TILE // 2, 1))
        hand[z, BAND:PACKED, t * TILE:(t + 1) * TILE] = jnp.where(left, low, high).astype(jnp.bfloat16)

    def ring_start(step):
        for part in range(2):
            for way in range(2):
                if part in ring_parts(way, step):
                    ring_copy(way, step, part).start()

    def ring_wait(step):
        for part in range(2):
            for way in range(2):
                if part in ring_parts(way, step):
                    ring_copy(way, step, part).wait_recv()

    def ring_on(step):
        for part in range(2):
            for way in range(2):
                if part in ring_parts(way, step):
                    ring_copy(way, step, part).wait_recv()
                if step < 3 and part in ring_parts(way, step + 1):
                    ring_copy(way, step + 1, part).start()

    def z_arrival(d):
        z_copy(d).wait_recv()
        for dy in (2, 1, 3):
            y_copy(d, dy).start()
        core_copy(d, 0).start()

    def y_arrival(d):
        for dy in (1, 3, 2):
            y_copy(d, dy).wait_recv()
            core_copy(d, dy).start()

    ring_start(0)
    for d in (1, 7, 2, 6):
        z_arrival(d)
    ring_on(0)
    y_arrival(0)
    for d in (3, 5, 4):
        z_arrival(d)
    y_arrival(1)
    y_arrival(7)
    ring_on(1)
    for dy in range(YS):
        for copy in stack_copies(dy):
            copy.wait_recv()
    for copy in pass_copies():
        copy.start()
    y_arrival(2)
    y_arrival(6)
    ring_on(2)
    for d in (3, 5, 4):
        y_arrival(d)

    for copy in pass_copies():
        copy.wait_recv()
    theirs = pivot.at[1 - c]
    remote(theirs, theirs, core_send, core_recv, at(dc=1)).wait_recv()

    eye = lax.broadcasted_iota(jnp.int32, (BAND, TILE), 0) == lax.broadcasted_iota(jnp.int32, (BAND, TILE), 1)

    def inverse_of(h):
        found = []
        for t in range(HALF // TILE):
            block = pivot[h, h * (ZS // 2) + t, :, :, t * TILE:(t + 1) * TILE].reshape(BAND, TILE)
            found.append(jnp.sum(jnp.where(eye, block.astype(jnp.float32), 0.0), axis=0, keepdims=True))
        return 1.0 / jnp.concatenate(found, axis=1)

    inverse = [inverse_of(h) for h in range(CORES)]
    present = [x < SLABS - 1, x > 0]

    def target(a, h):
        block = stacked[a, h].reshape(BAND, HALF).astype(jnp.float32)
        return jnp.where(present[a], block, 0.0)

    for a in range(2):
        for h in range(CORES):
            iterate[0, a * BAND:(a + 1) * BAND, h * HALF:(h + 1) * HALF] = (target(a, h) * inverse[h]).astype(jnp.bfloat16)
    for sweep in range(SWEEPS):
        now, later = sweep % 2, (sweep + 1) % 2
        for h in range(CORES):
            columns = slice(h * HALF, (h + 1) * HALF)
            product[...] = jnp.dot(iterate[now], pivot[h].reshape(ZS * BAND, HALF), preferred_element_type=jnp.float32)
            for a in range(2):
                rows = slice(a * BAND, (a + 1) * BAND)
                step = (target(a, h) - product[rows]) * inverse[h]
                iterate[later, rows, columns] = (iterate[now, rows, columns].astype(jnp.float32) + step).astype(jnp.bfloat16)

    ring_wait(3)
    for zs in range(ZS):
        for t in range(2):
            packed = hand[zs, BAND:PACKED, t * TILE:(t + 1) * TILE].astype(jnp.float32)
            turned = pltpu.roll(packed, TILE // 2, 1)
            sides_full[zs, 2 * t] = jnp.where(odd, turned, packed).astype(jnp.bfloat16)
            sides_full[zs, 2 * t + 1] = jnp.where(odd, packed, turned).astype(jnp.bfloat16)
    factor = iterate[SWEEPS % 2]
    coupled = jnp.dot(factor, hand[:, :BAND, :].reshape(ZS * BAND, 2 * TILE), preferred_element_type=jnp.float32)
    upper_part = jnp.where(present[0], coupled[:, :TILE], 0.0).astype(jnp.bfloat16)
    lower_part = jnp.where(present[1], coupled[:, TILE:], 0.0).astype(jnp.bfloat16)
    product[:, :TILE] = jnp.dot(factor, sides_full[...].reshape(ZS * BAND, TILE), preferred_element_type=jnp.float32)
    sides_part = product[:, :TILE].astype(jnp.bfloat16)
    for a in range(2):
        rows = slice(a * BAND, (a + 1) * BAND)
        update[0, a, :, :, 0:TILE] = upper_part[rows].reshape(YS, ROWS, TILE)
        update[0, a, :, :, TILE:2 * TILE] = lower_part[rows].reshape(YS, ROWS, TILE)
        update[0, a, :, :, 2 * TILE:] = sides_part[rows].reshape(YS, ROWS, TILE)

    def back_copy(a, dy):
        to = lax.rem(y + dy, YS)
        return remote(update.at[0, a, to], update.at[1, a, y], back_send.at[a, dy], back_recv.at[a, dy], at(dx=1 if a == 0 else 3, dy=dy))

    for dy in (2, 1, 3, 0):
        for a in range(2):
            back_copy(a, dy).start()
    for dy in range(YS):
        for a in range(2):
            back_copy(a, dy).wait_recv()

    for t in range(YS):
        columns = slice(t * TILE, (t + 1) * TILE)
        before, after = update[1, 0, t].astype(jnp.float32), update[1, 1, t].astype(jnp.float32)
        reduced = pivot_own[:, columns].astype(jnp.float32) - before[:, :TILE] - after[:, TILE:2 * TILE]
        pivot_out[:, columns] = reduced.astype(jnp.bfloat16)
        lower_out[:, columns] = (-before[:, TILE:2 * TILE]).astype(jnp.bfloat16)
        upper_out[:, columns] = (-after[:, :TILE]).astype(jnp.bfloat16)
    for t in range(2):
        columns = slice(t * TILE, (t + 1) * TILE)
        terms = [
            jnp.where(left, update[1, a, 2 * t, :, 2 * TILE:].astype(jnp.float32), update[1, a, 2 * t + 1, :, 2 * TILE:].astype(jnp.float32))
            for a in range(2)
        ]
        reduced = sides_own[:, columns].astype(jnp.float32) - terms[0] - terms[1]
        sides_out[:, columns] = reduced.astype(jnp.bfloat16)

    for d in NEAR_FIRST:
        z_copy(d).wait_send()
    for dy in range(1, YS):
        for copy in deal_copies(dy):
            copy.wait_send()
        for d in range(ZS):
            y_copy(d, dy).wait_send()
    for dy in range(YS):
        for copy in stack_copies(dy):
            copy.wait_send()
        for a in range(2):
            back_copy(a, dy).wait_send()
    for copy in pass_copies():
        copy.wait_send()
    mine = pivot.at[c]
    remote(mine, mine, core_send, core_recv, at(dc=1)).wait_send()
    for step in range(4):
        for way in range(2):
            for part in ring_parts(way, step):
                ring_copy(way, step, part).wait_send()


def hand_out(*refs):
    for src, dst in zip(refs[:4], refs[4:]):
        dst[...] = src[...]


def per_device(diagonals, lower, upper, sides):
    square = jax.ShapeDtypeStruct((ROWS, HALF), jnp.bfloat16)
    wide = jax.ShapeDtypeStruct((ROWS, HALF // 2), jnp.bfloat16)
    whole = pl.BlockSpec(memory_space=pltpu.VMEM)
    bf16 = jnp.bfloat16
    dma = pltpu.SemaphoreType.DMA
    outs = pl.pallas_call(
        kernel,
        out_shape=(square, square, square, wide),
        in_specs=[pl.BlockSpec(memory_space=pltpu.HBM)] * 4,
        out_specs=(whole,) * 4,
        scratch_shapes=[
            pltpu.VMEM((ROWS, HALF), bf16),
            pltpu.VMEM((ROWS, HALF), bf16),
            pltpu.VMEM((ROWS, HALF), bf16),
            pltpu.VMEM((ROWS, HALF // 2), bf16),
            pltpu.VMEM((CORES, ZS, YS, ROWS, HALF), bf16),
            pltpu.VMEM((2, CORES, YS, ROWS, HALF), bf16),
            pltpu.VMEM((YS, ROWS, TILE), bf16),
            pltpu.VMEM((ZS, PACKED, 2 * TILE), bf16),
            pltpu.VMEM((ZS, YS, ROWS, TILE), bf16),
            pltpu.VMEM((2, 2 * BAND, CORES * HALF), bf16),
            pltpu.VMEM((2 * BAND, HALF), jnp.float32),
            pltpu.VMEM((2, 2, YS, ROWS, 3 * TILE), bf16),
            dma((8,)),
            dma((ZS,)), dma((ZS,)),
            dma((ZS, YS)), dma((ZS, YS)),
            dma, dma,
            dma((2, YS)), dma((2, YS)),
            dma((2,)), dma((2,)),
            dma((YS, 3)), dma((YS, 3)),
            dma((2, 4, 2)), dma((2, 4, 2)),
            dma((2, YS)), dma((2, YS)),
        ],
        compiler_params=pltpu.CompilerParams(
            collective_id=0, has_side_effects=True, vmem_limit_bytes=60 * 2**20
        ),
    )(diagonals[0], lower[0], upper[0], sides[0])
    outs = pl.pallas_call(
        hand_out,
        out_shape=(square, square, square, wide),
        in_specs=[whole] * 4,
        out_specs=[whole] * 4,
        compiler_params=pltpu.CompilerParams(vmem_limit_bytes=60 * 2**20),
    )(*outs)
    return tuple(out[None] for out in outs)


def solution(mesh):
    spec = P("slab", "row", "col")
    return jax.shard_map(
        per_device, mesh=mesh, in_specs=(spec,) * 4, out_specs=(spec,) * 4, check_vma=False
    )
```

```python
import functools

import jax
import jax.numpy as jnp
from jax import lax
from jax.experimental import pallas as pl
from jax.experimental.pallas import tpu as pltpu
from jax.sharding import PartitionSpec as P

MESH = pl.DeviceIdType.MESH
SWEEPS = 2
SLABS, ZS, YS, CORES = 4, 8, 4, 2
ROWS = 32
HALF = 512
TILE = 128
BAND = YS * ROWS
PACKED = BAND + ROWS
Y_RELAYED = (0, 1, 7)
Z_RELAYED = ()
NEAR_FIRST = (1, 7, 2, 6, 3, 5, 4)


def kernel(
    pivot_in, lower_in, upper_in, sides_in,
    pivot_out, lower_out, upper_out, sides_out,
    pivot_own, lower_own, upper_own, sides_own,
    pivot, stacked, sides_raw, hand, sides_full, iterate, product, update,
    load_sem, z_send, z_recv, y_send, y_recv, core_send, core_recv,
    stack_send, stack_recv, pass_send, pass_recv, deal_send, deal_recv,
    band_send, band_recv, back_send, back_recv,
):
    x = lax.axis_index("slab")
    row = lax.axis_index("row")
    z, y = row // YS, row % YS
    c = lax.axis_index("col")

    def at(dx=0, dz=0, dy=0, dc=0):
        there = lax.rem(z + dz, ZS) * YS + lax.rem(y + dy, YS)
        return (lax.rem(x + dx, SLABS), there, lax.rem(c + dc, CORES))

    def remote(src, dst, send, recv, where):
        return pltpu.make_async_remote_copy(
            src_ref=src, dst_ref=dst, send_sem=send, recv_sem=recv,
            device_id=where, device_id_type=MESH,
        )

    def lanes(block, width=TILE):
        return pl.ds(pl.multiple_of(block * width, TILE), width)

    def band_rows(piece):
        return pl.ds(pl.multiple_of(piece * ROWS, ROWS), ROWS)

    loads = [
        pltpu.make_async_copy(pivot_in, pivot.at[c, z, y], load_sem.at[0]),
        pltpu.make_async_copy(upper_in, upper_own, load_sem.at[1]),
        pltpu.make_async_copy(lower_in, lower_own, load_sem.at[2]),
        pltpu.make_async_copy(sides_in, sides_own, load_sem.at[3]),
        pltpu.make_async_copy(upper_in.at[:, lanes(y)], hand.at[z, band_rows(y), pl.ds(0, TILE)], load_sem.at[4]),
        pltpu.make_async_copy(lower_in.at[:, lanes(y)], hand.at[z, band_rows(y), pl.ds(TILE, TILE)], load_sem.at[5]),
        pltpu.make_async_copy(sides_in.at[:, lanes(y // 2)], sides_raw.at[y], load_sem.at[6]),
        pltpu.make_async_copy(pivot_in, pivot_own, load_sem.at[7]),
    ]
    for load in loads:
        load.start()
    partners = [at(dz=d) for d in range(1, ZS)] + [at(dy=d) for d in range(1, YS)] + [at(dc=1)]
    partners += [at(dx=dx, dy=dy) for dx in (1, 3) for dy in range(YS)]
    barrier = pltpu.get_barrier_semaphore()
    for partner in partners:
        pl.semaphore_signal(barrier, inc=1, device_id=partner, device_id_type=MESH)
    for load in loads:
        load.wait()
    pl.semaphore_wait(barrier, len(partners))

    halves = (pl.ds(0, ROWS // 2), pl.ds(ROWS // 2, ROWS // 2))

    def z_copy(d):
        mine = pivot.at[c, z, y]
        return remote(mine, mine, z_send.at[d], z_recv.at[d], at(dz=d))

    def z_relay(d):
        way = 2 if d in (3, 4) else ZS - 2
        mine = pivot.at[c, lax.rem(z + ZS - way, ZS), y]
        if d in (0, 4):
            mine = mine.at[halves[d // 4]]
        return remote(mine, mine, z_send.at[d], z_recv.at[d], at(dz={3: 1, 4: 2, 5: ZS - 1, 0: ZS - 2}[d]))

    def y_copy(d, dy):
        zs = lax.rem(z + ZS - d, ZS)
        mine = pivot.at[c, zs, y]
        return remote(mine, mine, y_send.at[d, dy], y_recv.at[d, dy], at(dy=dy))

    def y_relay(d, dy):
        zs, ys = lax.rem(z + ZS - d, ZS), lax.rem(y + YS - dy, YS)
        piece = pivot.at[c, zs, ys].at[halves[dy // 2]]
        return remote(piece, piece, y_send.at[d, dy // 2 * 2], y_recv.at[d, dy // 2 * 2], at(dy=dy))

    def core_copy(d, dy):
        zs, ys = lax.rem(z + ZS - d, ZS), lax.rem(y + YS - dy, YS)
        mine = pivot.at[c, zs, ys]
        return remote(mine, mine, core_send, core_recv, at(dc=1))

    def deal_copies(dy):
        to = lax.rem(y + dy, YS)
        rows = band_rows(y)
        where = at(dy=dy)
        return [
            remote(upper_own.at[:, lanes(to)], hand.at[z, rows, pl.ds(0, TILE)], deal_send.at[dy, 0], deal_recv.at[dy, 0], where),
            remote(lower_own.at[:, lanes(to)], hand.at[z, rows, pl.ds(TILE, TILE)], deal_send.at[dy, 1], deal_recv.at[dy, 1], where),
            remote(sides_own.at[:, lanes(to // 2)], sides_raw.at[y], deal_send.at[dy, 2], deal_recv.at[dy, 2], where),
        ]

    def stack_copies(dy):
        return [
            remote(lower_own, stacked.at[0, c, y], stack_send.at[0, dy], stack_recv.at[0, dy], at(dx=3, dy=dy)),
            remote(upper_own, stacked.at[1, c, y], stack_send.at[1, dy], stack_recv.at[1, dy], at(dx=1, dy=dy)),
        ]

    def pass_copies():
        return [
            remote(stacked.at[a, c], stacked.at[a, c], pass_send.at[a], pass_recv.at[a], at(dc=1))
            for a in range(2)
        ]

    def band_copy(d, part):
        behind, ahead = {1: (0, 1), 7: (0, 7), 2: (0, 2), 6: (0, 6), 3: (2, 1), 5: (6, 7), 4: ((2, 2), (6, 6))[part]}[d]
        zs = lax.rem(z + ZS - behind, ZS)
        rows = hand.at[zs, pl.ds(part * (PACKED // 2), PACKED // 2)]
        return remote(rows, rows, band_send.at[d, part], band_recv.at[d, part], at(dz=ahead))

    for dy in (2, 1, 3):
        for copy in deal_copies(dy):
            copy.start()
    for d in NEAR_FIRST:
        if d not in Z_RELAYED:
            z_copy(d).start()
    core_copy(0, 0).start()
    for dy in (1, 3) if 0 in Y_RELAYED else (2, 1, 3):
        y_copy(0, dy).start()
    for dy in range(YS):
        for copy in stack_copies(dy):
            copy.start()

    lane = lax.broadcasted_iota(jnp.int32, (ROWS, TILE), 1)
    left = lane < TILE // 2
    odd = lax.rem(y, 2) == 1

    for dy in range(1, YS):
        for copy in deal_copies(dy):
            copy.wait_recv()
    for t in range(2):
        low = sides_raw[2 * t].astype(jnp.float32)
        high = sides_raw[2 * t + 1].astype(jnp.float32)
        low = jnp.where(odd, pltpu.roll(low, TILE // 2, 1), low)
        high = jnp.where(odd, high, pltpu.roll(high, TILE // 2, 1))
        hand[z, BAND:PACKED, t * TILE:(t + 1) * TILE] = jnp.where(left, low, high).astype(jnp.bfloat16)

    for d in (2, 6, 1, 7):
        for part in range(2):
            band_copy(d, part).start()

    def band_on():
        for part in range(2):
            for d, further in ((2, (3, 4)), (6, (5, 4))):
                band_copy(d, part).wait_recv()
                for on in further:
                    if on != 4 or part == (d == 6):
                        band_copy(on, part).start()

    def z_arrival(d):
        if d in Z_RELAYED:
            z_relay(d).wait_recv()
            if d == 4:
                z_relay(0).wait_recv()
        else:
            z_copy(d).wait_recv()
        if d in (2, 6) and Z_RELAYED:
            for further in ((3, 4) if d == 2 else (5, 0)):
                z_relay(further).start()
        for dy in (1, 3) if d in Y_RELAYED else (2, 1, 3):
            y_copy(d, dy).start()
        core_copy(d, 0).start()

    def y_arrival(d):
        for dy in (1, 3):
            y_copy(d, dy).wait_recv()
            if d in Y_RELAYED:
                y_relay(d, dy).start()
            core_copy(d, dy).start()
        if d not in Y_RELAYED:
            y_copy(d, 2).wait_recv()
            core_copy(d, 2).start()

    def y_last(d):
        if d in Y_RELAYED:
            y_relay(d, 1).wait_recv()
            y_relay(d, 3).wait_recv()
            core_copy(d, 2).start()

    z_arrival(1)
    z_arrival(7)
    z_arrival(2)
    z_arrival(6)
    y_arrival(0)
    z_arrival(3)
    z_arrival(5)
    z_arrival(4)
    band_on()
    y_arrival(1)
    y_arrival(7)
    y_last(0)
    for dy in range(YS):
        for copy in stack_copies(dy):
            copy.wait_recv()
    for copy in pass_copies():
        copy.start()
    y_arrival(2)
    y_arrival(6)
    y_last(1)
    y_last(7)
    y_arrival(3)
    y_arrival(5)
    y_arrival(4)
    y_last(2)
    y_last(6)
    y_last(3)
    y_last(5)
    y_last(4)

    for copy in pass_copies():
        copy.wait_recv()
    theirs = pivot.at[1 - c]
    remote(theirs, theirs, core_send, core_recv, at(dc=1)).wait_recv()

    eye = lax.broadcasted_iota(jnp.int32, (BAND, TILE), 0) == lax.broadcasted_iota(jnp.int32, (BAND, TILE), 1)

    def inverse_of(h):
        found = []
        for t in range(HALF // TILE):
            block = pivot[h, h * (ZS // 2) + t, :, :, t * TILE:(t + 1) * TILE].reshape(BAND, TILE)
            found.append(jnp.sum(jnp.where(eye, block.astype(jnp.float32), 0.0), axis=0, keepdims=True))
        return 1.0 / jnp.concatenate(found, axis=1)

    inverse = [inverse_of(h) for h in range(CORES)]
    present = [x < SLABS - 1, x > 0]

    def target(a, h):
        block = stacked[a, h].reshape(BAND, HALF).astype(jnp.float32)
        return jnp.where(present[a], block, 0.0)

    for a in range(2):
        for h in range(CORES):
            iterate[0, a * BAND:(a + 1) * BAND, h * HALF:(h + 1) * HALF] = (target(a, h) * inverse[h]).astype(jnp.bfloat16)
    for sweep in range(SWEEPS):
        now, later = sweep % 2, (sweep + 1) % 2
        for h in range(CORES):
            columns = slice(h * HALF, (h + 1) * HALF)
            product[...] = jnp.dot(iterate[now], pivot[h].reshape(ZS * BAND, HALF), preferred_element_type=jnp.float32)
            for a in range(2):
                rows = slice(a * BAND, (a + 1) * BAND)
                step = (target(a, h) - product[rows]) * inverse[h]
                iterate[later, rows, columns] = (iterate[now, rows, columns].astype(jnp.float32) + step).astype(jnp.bfloat16)

    for d in (1, 7, 3, 5, 4):
        for part in range(2):
            band_copy(d, part).wait_recv()
    for zs in range(ZS):
        for t in range(2):
            packed = hand[zs, BAND:PACKED, t * TILE:(t + 1) * TILE].astype(jnp.float32)
            turned = pltpu.roll(packed, TILE // 2, 1)
            sides_full[zs, 2 * t] = jnp.where(odd, turned, packed).astype(jnp.bfloat16)
            sides_full[zs, 2 * t + 1] = jnp.where(odd, packed, turned).astype(jnp.bfloat16)
    factor = iterate[SWEEPS % 2]
    coupled = jnp.dot(factor, hand[:, :BAND, :].reshape(ZS * BAND, 2 * TILE), preferred_element_type=jnp.float32)
    upper_part = jnp.where(present[0], coupled[:, :TILE], 0.0).astype(jnp.bfloat16)
    lower_part = jnp.where(present[1], coupled[:, TILE:], 0.0).astype(jnp.bfloat16)
    product[:, :TILE] = jnp.dot(factor, sides_full[...].reshape(ZS * BAND, TILE), preferred_element_type=jnp.float32)
    sides_part = product[:, :TILE].astype(jnp.bfloat16)
    for a in range(2):
        rows = slice(a * BAND, (a + 1) * BAND)
        update[0, a, :, :, 0:TILE] = upper_part[rows].reshape(YS, ROWS, TILE)
        update[0, a, :, :, TILE:2 * TILE] = lower_part[rows].reshape(YS, ROWS, TILE)
        update[0, a, :, :, 2 * TILE:] = sides_part[rows].reshape(YS, ROWS, TILE)

    def back_copy(a, dy):
        to = lax.rem(y + dy, YS)
        return remote(update.at[0, a, to], update.at[1, a, y], back_send.at[a, dy], back_recv.at[a, dy], at(dx=1 if a == 0 else 3, dy=dy))

    for dy in (2, 1, 3, 0):
        for a in range(2):
            back_copy(a, dy).start()
    for dy in range(YS):
        for a in range(2):
            back_copy(a, dy).wait_recv()

    for t in range(YS):
        columns = slice(t * TILE, (t + 1) * TILE)
        before, after = update[1, 0, t].astype(jnp.float32), update[1, 1, t].astype(jnp.float32)
        reduced = pivot_own[:, columns].astype(jnp.float32) - before[:, :TILE] - after[:, TILE:2 * TILE]
        pivot_out[:, columns] = reduced.astype(jnp.bfloat16)
        lower_out[:, columns] = (-before[:, TILE:2 * TILE]).astype(jnp.bfloat16)
        upper_out[:, columns] = (-after[:, :TILE]).astype(jnp.bfloat16)
    for t in range(2):
        columns = slice(t * TILE, (t + 1) * TILE)
        terms = [
            jnp.where(left, update[1, a, 2 * t, :, 2 * TILE:].astype(jnp.float32), update[1, a, 2 * t + 1, :, 2 * TILE:].astype(jnp.float32))
            for a in range(2)
        ]
        reduced = sides_own[:, columns].astype(jnp.float32) - terms[0] - terms[1]
        sides_out[:, columns] = reduced.astype(jnp.bfloat16)

    for d in NEAR_FIRST:
        if d not in Z_RELAYED:
            z_copy(d).wait_send()
    for d in (3, 5, 4, 0) if Z_RELAYED else ():
        z_relay(d).wait_send()
    for dy in range(1, YS):
        for copy in deal_copies(dy):
            copy.wait_send()
        for d in range(ZS):
            if d not in Y_RELAYED or dy != 2:
                y_copy(d, dy).wait_send()
            if d in Y_RELAYED and dy != 2:
                y_relay(d, dy).wait_send()
    for dy in range(YS):
        for copy in stack_copies(dy):
            copy.wait_send()
        for a in range(2):
            back_copy(a, dy).wait_send()
    for copy in pass_copies():
        copy.wait_send()
    mine = pivot.at[c]
    remote(mine, mine, core_send, core_recv, at(dc=1)).wait_send()
    for d in range(1, ZS):
        for part in range(2):
            band_copy(d, part).wait_send()


def hand_out(*refs):
    sources, results, sem = refs[:4], refs[4:8], refs[8]
    copies = [pltpu.make_async_copy(src, dst, sem.at[i]) for i, (src, dst) in enumerate(zip(sources, results))]
    for copy in copies:
        copy.start()
    for copy in copies:
        copy.wait()


def per_device(diagonals, lower, upper, sides):
    square = jax.ShapeDtypeStruct((ROWS, HALF), jnp.bfloat16)
    wide = jax.ShapeDtypeStruct((ROWS, HALF // 2), jnp.bfloat16)
    whole = pl.BlockSpec(memory_space=pltpu.VMEM)
    bf16 = jnp.bfloat16
    dma = pltpu.SemaphoreType.DMA
    outs = pl.pallas_call(
        kernel,
        out_shape=(square, square, square, wide),
        in_specs=[pl.BlockSpec(memory_space=pltpu.HBM)] * 4,
        out_specs=(whole,) * 4,
        scratch_shapes=[
            pltpu.VMEM((ROWS, HALF), bf16),
            pltpu.VMEM((ROWS, HALF), bf16),
            pltpu.VMEM((ROWS, HALF), bf16),
            pltpu.VMEM((ROWS, HALF // 2), bf16),
            pltpu.VMEM((CORES, ZS, YS, ROWS, HALF), bf16),
            pltpu.VMEM((2, CORES, YS, ROWS, HALF), bf16),
            pltpu.VMEM((YS, ROWS, TILE), bf16),
            pltpu.VMEM((ZS, PACKED, 2 * TILE), bf16),
            pltpu.VMEM((ZS, YS, ROWS, TILE), bf16),
            pltpu.VMEM((2, 2 * BAND, CORES * HALF), bf16),
            pltpu.VMEM((2 * BAND, HALF), jnp.float32),
            pltpu.VMEM((2, 2, YS, ROWS, 3 * TILE), bf16),
            dma((8,)),
            dma((ZS,)), dma((ZS,)),
            dma((ZS, YS)), dma((ZS, YS)),
            dma, dma,
            dma((2, YS)), dma((2, YS)),
            dma((2,)), dma((2,)),
            dma((YS, 3)), dma((YS, 3)),
            dma((ZS, 2)), dma((ZS, 2)),
            dma((2, YS)), dma((2, YS)),
        ],
        compiler_params=pltpu.CompilerParams(
            collective_id=0, has_side_effects=True, vmem_limit_bytes=55104 * 2**10
        ),
    )(diagonals[0], lower[0], upper[0], sides[0])
    outs = pl.pallas_call(
        hand_out,
        out_shape=(square, square, square, wide),
        in_specs=[pl.BlockSpec(memory_space=pl.ANY)] * 4,
        out_specs=[pl.BlockSpec(memory_space=pl.ANY)] * 4,
        scratch_shapes=[dma((4,))],
        compiler_params=pltpu.CompilerParams(vmem_limit_bytes=55104 * 2**10),
    )(*outs)
    return tuple(out[None] for out in outs)


def solution(mesh):
    spec = P("slab", "row", "col")
    return jax.shard_map(
        per_device, mesh=mesh, in_specs=(spec,) * 4, out_specs=(spec,) * 4, check_vma=False
    )
```

```python
import functools

import jax
import jax.numpy as jnp
from jax import lax
from jax.experimental import pallas as pl
from jax.experimental.pallas import tpu as pltpu
from jax.sharding import PartitionSpec as P

MESH = pl.DeviceIdType.MESH
SWEEPS = 2
SLABS, ZS, YS, CORES = 4, 8, 4, 2
ROWS = 32
HALF = 512
TILE = 128
BAND = YS * ROWS
PACKED = BAND + ROWS
NEAR_FIRST = (1, 7, 2, 6, 3, 5, 4)


def kernel(
    pivot_in, lower_in, upper_in, sides_in,
    pivot_out, lower_out, upper_out, sides_out,
    pivot_own, lower_own, upper_own, sides_own,
    pivot, stacked, sides_raw, hand, sides_full, iterate, product, update,
    load_sem, z_send, z_recv, y_send, y_recv, core_send, core_recv,
    stack_send, stack_recv, pass_send, pass_recv, deal_send, deal_recv,
    band_send, band_recv, back_send, back_recv,
):
    x = lax.axis_index("slab")
    row = lax.axis_index("row")
    z, y = row // YS, row % YS
    c = lax.axis_index("col")

    def at(dx=0, dz=0, dy=0, dc=0):
        there = lax.rem(z + dz, ZS) * YS + lax.rem(y + dy, YS)
        return (lax.rem(x + dx, SLABS), there, lax.rem(c + dc, CORES))

    def remote(src, dst, send, recv, where):
        return pltpu.make_async_remote_copy(
            src_ref=src, dst_ref=dst, send_sem=send, recv_sem=recv,
            device_id=where, device_id_type=MESH,
        )

    def lanes(block, width=TILE):
        return pl.ds(pl.multiple_of(block * width, TILE), width)

    def band_rows(piece):
        return pl.ds(pl.multiple_of(piece * ROWS, ROWS), ROWS)

    loads = [
        pltpu.make_async_copy(pivot_in, pivot.at[c, z, y], load_sem.at[0]),
        pltpu.make_async_copy(upper_in, upper_own, load_sem.at[1]),
        pltpu.make_async_copy(lower_in, lower_own, load_sem.at[2]),
        pltpu.make_async_copy(sides_in, sides_own, load_sem.at[3]),
        pltpu.make_async_copy(upper_in.at[:, lanes(y)], hand.at[z, band_rows(y), pl.ds(0, TILE)], load_sem.at[4]),
        pltpu.make_async_copy(lower_in.at[:, lanes(y)], hand.at[z, band_rows(y), pl.ds(TILE, TILE)], load_sem.at[5]),
        pltpu.make_async_copy(sides_in.at[:, lanes(y // 2)], sides_raw.at[y], load_sem.at[6]),
        pltpu.make_async_copy(pivot_in, pivot_own, load_sem.at[7]),
    ]
    for load in loads:
        load.start()
    partners = [at(dz=d) for d in range(1, ZS)] + [at(dy=d) for d in range(1, YS)] + [at(dc=1)]
    partners += [at(dx=dx, dy=dy) for dx in (1, 3) for dy in range(YS)]
    barrier = pltpu.get_barrier_semaphore()
    for partner in partners:
        pl.semaphore_signal(barrier, inc=1, device_id=partner, device_id_type=MESH)
    for load in loads:
        load.wait()
    pl.semaphore_wait(barrier, len(partners))

    def sent(ref, sem):
        remote(ref, ref, sem, core_recv, at(dc=1)).wait_send()

    def arrived(ref, sem):
        remote(ref, ref, core_send, sem, at(dc=1)).wait_recv()

    def z_copy(d):
        mine = pivot.at[c, z, y]
        return remote(mine, mine, z_send, z_recv.at[d], at(dz=d))

    def y_copy(d, dy):
        mine = pivot.at[c, lax.rem(z + ZS - d, ZS), y]
        return remote(mine, mine, y_send, y_recv.at[d], at(dy=dy))

    def core_copy(d):
        mine = pivot.at[c, lax.rem(z + ZS - d, ZS)]
        return remote(mine, mine, core_send, core_recv, at(dc=1))

    def deal_copies(dy):
        to = lax.rem(y + dy, YS)
        rows = band_rows(y)
        where = at(dy=dy)
        return [
            remote(upper_own.at[:, lanes(to)], hand.at[z, rows, pl.ds(0, TILE)], deal_send.at[0], deal_recv.at[0], where),
            remote(lower_own.at[:, lanes(to)], hand.at[z, rows, pl.ds(TILE, TILE)], deal_send.at[1], deal_recv.at[1], where),
            remote(sides_own.at[:, lanes(to // 2)], sides_raw.at[y], deal_send.at[2], deal_recv.at[2], where),
        ]

    def stack_copies(dy):
        return [
            remote(lower_own, stacked.at[0, c, y], stack_send, stack_recv, at(dx=3, dy=dy)),
            remote(upper_own, stacked.at[1, c, y], stack_send, stack_recv, at(dx=1, dy=dy)),
        ]

    def pass_copies():
        return [
            remote(stacked.at[a, c], stacked.at[a, c], pass_send.at[a], pass_recv.at[a], at(dc=1))
            for a in range(2)
        ]

    def band_copy(d, part=None):
        behind, ahead = {1: (0, 1), 7: (0, 7), 2: (0, 2), 6: (0, 6), 3: (2, 1), 5: (6, 7), 4: ((2, 2), (6, 6))[part or 0]}[d]
        zs = lax.rem(z + ZS - behind, ZS)
        rows = hand.at[zs] if part is None else hand.at[zs, pl.ds(part * (PACKED // 2), PACKED // 2)]
        return remote(rows, rows, band_send, band_recv.at[d if d in (2, 6) else 0], at(dz=ahead))

    for dy in (2, 1, 3):
        for copy in deal_copies(dy):
            copy.start()
    for d in NEAR_FIRST:
        z_copy(d).start()
    for dy in (2, 1, 3):
        y_copy(0, dy).start()
    for dy in range(YS):
        for copy in stack_copies(dy):
            copy.start()

    lane = lax.broadcasted_iota(jnp.int32, (ROWS, TILE), 1)
    left = lane < TILE // 2
    odd = lax.rem(y, 2) == 1

    for kind in range(3):
        arrived(sides_raw.at[pl.ds(0, YS - 1)], deal_recv.at[kind])
    for t in range(2):
        low = sides_raw[2 * t].astype(jnp.float32)
        high = sides_raw[2 * t + 1].astype(jnp.float32)
        low = jnp.where(odd, pltpu.roll(low, TILE // 2, 1), low)
        high = jnp.where(odd, high, pltpu.roll(high, TILE // 2, 1))
        hand[z, BAND:PACKED, t * TILE:(t + 1) * TILE] = jnp.where(left, low, high).astype(jnp.bfloat16)

    for d in (2, 6, 1, 7):
        band_copy(d).start()

    def z_arrival(d):
        z_copy(d).wait_recv()
        for dy in (2, 1, 3):
            y_copy(d, dy).start()

    def y_arrival(d):
        arrived(pivot.at[c, 0, pl.ds(0, YS - 1)], y_recv.at[d])
        core_copy(d).start()

    for d in (1, 7, 2, 6):
        z_arrival(d)
    y_arrival(0)
    for d in (3, 5, 4):
        z_arrival(d)
    y_arrival(1)
    y_arrival(7)
    for d, further, half in ((2, 3, 0), (6, 5, 1)):
        band_copy(d).wait_recv()
        band_copy(further).start()
        band_copy(4, half).start()
    arrived(stacked.at[:, c], stack_recv)
    for copy in pass_copies():
        copy.start()
    for d in (2, 6, 3, 5, 4):
        y_arrival(d)
    for copy in pass_copies():
        copy.wait_recv()
    arrived(pivot.at[1 - c], core_recv)

    eye = lax.broadcasted_iota(jnp.int32, (BAND, TILE), 0) == lax.broadcasted_iota(jnp.int32, (BAND, TILE), 1)

    def inverse_of(h):
        found = []
        for t in range(HALF // TILE):
            block = pivot[h, h * (ZS // 2) + t, :, :, t * TILE:(t + 1) * TILE].reshape(BAND, TILE)
            found.append(jnp.sum(jnp.where(eye, block.astype(jnp.float32), 0.0), axis=0, keepdims=True))
        return 1.0 / jnp.concatenate(found, axis=1)

    inverse = [inverse_of(h) for h in range(CORES)]
    present = [x < SLABS - 1, x > 0]

    def target(a, h):
        block = stacked[a, h].reshape(BAND, HALF).astype(jnp.float32)
        return jnp.where(present[a], block, 0.0)

    for a in range(2):
        for h in range(CORES):
            iterate[0, a * BAND:(a + 1) * BAND, h * HALF:(h + 1) * HALF] = (target(a, h) * inverse[h]).astype(jnp.bfloat16)
    for sweep in range(SWEEPS):
        now, later = sweep % 2, (sweep + 1) % 2
        for h in range(CORES):
            columns = slice(h * HALF, (h + 1) * HALF)
            product[...] = jnp.dot(iterate[now], pivot[h].reshape(ZS * BAND, HALF), preferred_element_type=jnp.float32)
            for a in range(2):
                rows = slice(a * BAND, (a + 1) * BAND)
                step = (target(a, h) - product[rows]) * inverse[h]
                iterate[later, rows, columns] = (iterate[now, rows, columns].astype(jnp.float32) + step).astype(jnp.bfloat16)

    arrived(hand.at[pl.ds(0, 5)], band_recv.at[0])
    for zs in range(ZS):
        for t in range(2):
            packed = hand[zs, BAND:PACKED, t * TILE:(t + 1) * TILE].astype(jnp.float32)
            turned = pltpu.roll(packed, TILE // 2, 1)
            sides_full[zs, 2 * t] = jnp.where(odd, turned, packed).astype(jnp.bfloat16)
            sides_full[zs, 2 * t + 1] = jnp.where(odd, packed, turned).astype(jnp.bfloat16)
    factor = iterate[SWEEPS % 2]
    coupled = jnp.dot(factor, hand[:, :BAND, :].reshape(ZS * BAND, 2 * TILE), preferred_element_type=jnp.float32)
    upper_part = jnp.where(present[0], coupled[:, :TILE], 0.0).astype(jnp.bfloat16)
    lower_part = jnp.where(present[1], coupled[:, TILE:], 0.0).astype(jnp.bfloat16)
    product[:, :TILE] = jnp.dot(factor, sides_full[...].reshape(ZS * BAND, TILE), preferred_element_type=jnp.float32)
    sides_part = product[:, :TILE].astype(jnp.bfloat16)
    for a in range(2):
        rows = slice(a * BAND, (a + 1) * BAND)
        update[0, a, :, :, 0:TILE] = upper_part[rows].reshape(YS, ROWS, TILE)
        update[0, a, :, :, TILE:2 * TILE] = lower_part[rows].reshape(YS, ROWS, TILE)
        update[0, a, :, :, 2 * TILE:] = sides_part[rows].reshape(YS, ROWS, TILE)

    def back_copy(a, dy):
        to = lax.rem(y + dy, YS)
        return remote(update.at[0, a, to], update.at[1, a, y], back_send, back_recv, at(dx=1 if a == 0 else 3, dy=dy))

    for dy in (2, 1, 3, 0):
        for a in range(2):
            back_copy(a, dy).start()
    arrived(update.at[1], back_recv)

    for t in range(YS):
        columns = slice(t * TILE, (t + 1) * TILE)
        before, after = update[1, 0, t].astype(jnp.float32), update[1, 1, t].astype(jnp.float32)
        reduced = pivot_own[:, columns].astype(jnp.float32) - before[:, :TILE] - after[:, TILE:2 * TILE]
        pivot_out[:, columns] = reduced.astype(jnp.bfloat16)
        lower_out[:, columns] = (-before[:, TILE:2 * TILE]).astype(jnp.bfloat16)
        upper_out[:, columns] = (-after[:, :TILE]).astype(jnp.bfloat16)
    for t in range(2):
        columns = slice(t * TILE, (t + 1) * TILE)
        terms = [
            jnp.where(left, update[1, a, 2 * t, :, 2 * TILE:].astype(jnp.float32), update[1, a, 2 * t + 1, :, 2 * TILE:].astype(jnp.float32))
            for a in range(2)
        ]
        reduced = sides_own[:, columns].astype(jnp.float32) - terms[0] - terms[1]
        sides_out[:, columns] = reduced.astype(jnp.bfloat16)

    sent(pivot.at[c, pl.ds(0, ZS - 1), 0], z_send)
    sent(pivot.at[c, pl.ds(0, 6)], y_send)
    sent(pivot.at[c], core_send)
    sent(stacked.at[:, c], stack_send)
    for copy in pass_copies():
        copy.wait_send()
    for kind in range(3):
        sent(sides_raw.at[pl.ds(0, YS - 1)], deal_send.at[kind])
    sent(hand.at[pl.ds(0, ZS - 1)], band_send)
    sent(update.at[0], back_send)


def hand_out(*refs):
    sources, results, sem = refs[:4], refs[4:8], refs[8]
    copies = [pltpu.make_async_copy(src, dst, sem.at[i]) for i, (src, dst) in enumerate(zip(sources, results))]
    for copy in copies:
        copy.start()
    for copy in copies:
        copy.wait()


def per_device(diagonals, lower, upper, sides):
    square = jax.ShapeDtypeStruct((ROWS, HALF), jnp.bfloat16)
    wide = jax.ShapeDtypeStruct((ROWS, HALF // 2), jnp.bfloat16)
    whole = pl.BlockSpec(memory_space=pltpu.VMEM)
    bf16 = jnp.bfloat16
    dma = pltpu.SemaphoreType.DMA
    outs = pl.pallas_call(
        kernel,
        out_shape=(square, square, square, wide),
        in_specs=[pl.BlockSpec(memory_space=pltpu.HBM)] * 4,
        out_specs=(whole,) * 4,
        scratch_shapes=[
            pltpu.VMEM((ROWS, HALF), bf16),
            pltpu.VMEM((ROWS, HALF), bf16),
            pltpu.VMEM((ROWS, HALF), bf16),
            pltpu.VMEM((ROWS, HALF // 2), bf16),
            pltpu.VMEM((CORES, ZS, YS, ROWS, HALF), bf16),
            pltpu.VMEM((2, CORES, YS, ROWS, HALF), bf16),
            pltpu.VMEM((YS, ROWS, TILE), bf16),
            pltpu.VMEM((ZS, PACKED, 2 * TILE), bf16),
            pltpu.VMEM((ZS, YS, ROWS, TILE), bf16),
            pltpu.VMEM((2, 2 * BAND, CORES * HALF), bf16),
            pltpu.VMEM((2 * BAND, HALF), jnp.float32),
            pltpu.VMEM((2, 2, YS, ROWS, 3 * TILE), bf16),
            dma((8,)),
            dma, dma((ZS,)),
            dma, dma((ZS,)),
            dma, dma,
            dma, dma,
            dma((2,)), dma((2,)),
            dma((3,)), dma((3,)),
            dma, dma((ZS,)),
            dma, dma,
        ],
        compiler_params=pltpu.CompilerParams(
            collective_id=0, has_side_effects=True, vmem_limit_bytes=55104 * 2**10
        ),
    )(*(pltpu.with_memory_space_constraint(array[0], pltpu.HBM) for array in (diagonals, lower, upper, sides)))
    outs = pl.pallas_call(
        hand_out,
        out_shape=(square, square, square, wide),
        in_specs=[pl.BlockSpec(memory_space=pl.ANY)] * 4,
        out_specs=[pl.BlockSpec(memory_space=pl.ANY)] * 4,
        scratch_shapes=[dma((4,))],
        compiler_params=pltpu.CompilerParams(vmem_limit_bytes=55104 * 2**10),
    )(*outs)
    return tuple(out[None] for out in outs)


def solution(mesh):
    spec = P("slab", "row", "col")
    return jax.shard_map(
        per_device, mesh=mesh, in_specs=(spec,) * 4, out_specs=(spec,) * 4, check_vma=False
    )
```

```python
import functools

import jax
import jax.numpy as jnp
from jax import lax
from jax.experimental import pallas as pl
from jax.experimental.pallas import tpu as pltpu
from jax.sharding import PartitionSpec as P

MESH = pl.DeviceIdType.MESH
SWEEPS = 2
SLABS, ZS, YS, CORES = 4, 8, 4, 2
ROWS = 32
HALF = 512
TILE = 128
BAND = YS * ROWS
PACKED = BAND + ROWS
NEAR_FIRST = (1, 7, 2, 6, 3, 5, 4)


def kernel(
    pivot_in, lower_in, upper_in, sides_in,
    pivot_out, lower_out, upper_out, sides_out,
    pivot_own, lower_own, upper_own, sides_own,
    pivot, stacked, sides_raw, hand, sides_full, iterate, product, update,
    load_sem, z_send, z_recv, y_send, y_recv, core_send, core_recv,
    stack_send, stack_recv, pass_send, pass_recv, deal_send, deal_recv,
    band_send, band_recv, back_send, back_recv,
):
    x = lax.axis_index("slab")
    row = lax.axis_index("row")
    z, y = row // YS, row % YS
    c = lax.axis_index("col")

    def at(dx=0, dz=0, dy=0, dc=0):
        there = lax.rem(z + dz, ZS) * YS + lax.rem(y + dy, YS)
        return (lax.rem(x + dx, SLABS), there, lax.rem(c + dc, CORES))

    def remote(src, dst, send, recv, where):
        return pltpu.make_async_remote_copy(
            src_ref=src, dst_ref=dst, send_sem=send, recv_sem=recv,
            device_id=where, device_id_type=MESH,
        )

    def lanes(block, width=TILE):
        return pl.ds(pl.multiple_of(block * width, TILE), width)

    def band_rows(piece):
        return pl.ds(pl.multiple_of(piece * ROWS, ROWS), ROWS)

    loads = [
        pltpu.make_async_copy(pivot_in, pivot.at[c, z, y], load_sem.at[0]),
        pltpu.make_async_copy(upper_in, upper_own, load_sem.at[1]),
        pltpu.make_async_copy(lower_in, lower_own, load_sem.at[2]),
        pltpu.make_async_copy(sides_in, sides_own, load_sem.at[3]),
        pltpu.make_async_copy(upper_in.at[:, lanes(y)], hand.at[z, band_rows(y), pl.ds(0, TILE)], load_sem.at[4]),
        pltpu.make_async_copy(lower_in.at[:, lanes(y)], hand.at[z, band_rows(y), pl.ds(TILE, TILE)], load_sem.at[5]),
        pltpu.make_async_copy(sides_in.at[:, lanes(y // 2)], sides_raw.at[y], load_sem.at[6]),
        pltpu.make_async_copy(pivot_in, pivot_own, load_sem.at[7]),
    ]
    for load in loads:
        load.start()
    partners = [at(dz=d) for d in range(1, ZS)] + [at(dy=d) for d in range(1, YS)] + [at(dc=1)]
    present = [x < SLABS - 1, x > 0]
    barrier = pltpu.get_barrier_semaphore()
    for partner in partners:
        pl.semaphore_signal(barrier, inc=1, device_id=partner, device_id_type=MESH)
    for there, dx in zip(present, (1, SLABS - 1)):
        @pl.when(there)
        def greet(dx=dx):
            for dy in range(YS):
                pl.semaphore_signal(barrier, inc=1, device_id=at(dx=dx, dy=dy), device_id_type=MESH)

    for load in loads:
        load.wait()
    neighbours = present[0].astype(jnp.int32) + present[1].astype(jnp.int32)
    pl.semaphore_wait(barrier, len(partners) + YS * neighbours)

    for a in range(2):
        @pl.when(jnp.logical_not(present[a]))
        def no_stack(a=a):
            stacked[a] = jnp.zeros(stacked.shape[1:], jnp.bfloat16)
            update[1, 1 - a] = jnp.zeros(update.shape[2:], jnp.bfloat16)


    def sent(ref, sem):
        remote(ref, ref, sem, core_recv, at(dc=1)).wait_send()

    def arrived(ref, sem):
        remote(ref, ref, core_send, sem, at(dc=1)).wait_recv()

    def z_copy(d):
        mine = pivot.at[c, z, y]
        return remote(mine, mine, z_send, z_recv.at[d], at(dz=d))

    def y_copy(d, dy):
        mine = pivot.at[c, lax.rem(z + ZS - d, ZS), y]
        return remote(mine, mine, y_send, y_recv.at[d], at(dy=dy))

    def core_copy(d):
        mine = pivot.at[c, lax.rem(z + ZS - d, ZS)]
        return remote(mine, mine, core_send, core_recv, at(dc=1))

    def deal_copies(dy):
        to = lax.rem(y + dy, YS)
        rows = band_rows(y)
        where = at(dy=dy)
        return [
            remote(upper_own.at[:, lanes(to)], hand.at[z, rows, pl.ds(0, TILE)], deal_send.at[0], deal_recv.at[0], where),
            remote(lower_own.at[:, lanes(to)], hand.at[z, rows, pl.ds(TILE, TILE)], deal_send.at[1], deal_recv.at[1], where),
            remote(sides_own.at[:, lanes(to // 2)], sides_raw.at[y], deal_send.at[2], deal_recv.at[2], where),
        ]

    def stack_copy(a, dy):
        source, dx = ((lower_own, SLABS - 1), (upper_own, 1))[a]
        return remote(source, stacked.at[a, c, y], stack_send.at[a], stack_recv.at[a], at(dx=dx, dy=dy))

    def pass_copy(a):
        return remote(stacked.at[a, c], stacked.at[a, c], pass_send.at[a], pass_recv.at[a], at(dc=1))

    def band_copy(d, part=None):
        behind, ahead = {1: (0, 1), 7: (0, 7), 2: (0, 2), 6: (0, 6), 3: (2, 1), 5: (6, 7), 4: ((2, 2), (6, 6))[part or 0]}[d]
        zs = lax.rem(z + ZS - behind, ZS)
        rows = hand.at[zs] if part is None else hand.at[zs, pl.ds(part * (PACKED // 2), PACKED // 2)]
        return remote(rows, rows, band_send, band_recv.at[d if d in (2, 6) else 0], at(dz=ahead))

    for dy in (2, 1, 3):
        for copy in deal_copies(dy):
            copy.start()
    for d in NEAR_FIRST:
        z_copy(d).start()
    for dy in (2, 1, 3):
        y_copy(0, dy).start()
    for a in range(2):
        @pl.when(present[1 - a])
        def stack_start(a=a):
            for dy in range(YS):
                stack_copy(a, dy).start()

    lane = lax.broadcasted_iota(jnp.int32, (ROWS, TILE), 1)
    left = lane < TILE // 2
    odd = lax.rem(y, 2) == 1

    for kind in range(3):
        arrived(sides_raw.at[pl.ds(0, YS - 1)], deal_recv.at[kind])
    for t in range(2):
        low = sides_raw[2 * t].astype(jnp.float32)
        high = sides_raw[2 * t + 1].astype(jnp.float32)
        low = jnp.where(odd, pltpu.roll(low, TILE // 2, 1), low)
        high = jnp.where(odd, high, pltpu.roll(high, TILE // 2, 1))
        hand[z, BAND:PACKED, t * TILE:(t + 1) * TILE] = jnp.where(left, low, high).astype(jnp.bfloat16)

    for d in (2, 6, 1, 7):
        band_copy(d).start()

    def z_arrival(d):
        z_copy(d).wait_recv()
        for dy in (2, 1, 3):
            y_copy(d, dy).start()

    def y_arrival(d):
        arrived(pivot.at[c, 0, pl.ds(0, YS - 1)], y_recv.at[d])
        core_copy(d).start()

    for d in (1, 7, 2, 6):
        z_arrival(d)
    y_arrival(0)
    for d in (3, 5, 4):
        z_arrival(d)
    y_arrival(1)
    y_arrival(7)
    for d, further, half in ((2, 3, 0), (6, 5, 1)):
        band_copy(d).wait_recv()
        band_copy(further).start()
        band_copy(4, half).start()
    y_arrival(2)
    y_arrival(6)
    for a in range(2):
        @pl.when(present[a])
        def stack_on(a=a):
            arrived(stacked.at[a, c], stack_recv.at[a])
            pass_copy(a).start()

    for d in (3, 5, 4):
        y_arrival(d)
    arrived(hand.at[pl.ds(0, 5)], band_recv.at[0])
    for zs in range(ZS):
        for t in range(2):
            packed = hand[zs, BAND:PACKED, t * TILE:(t + 1) * TILE].astype(jnp.float32)
            turned = pltpu.roll(packed, TILE // 2, 1)
            sides_full[zs, 2 * t] = jnp.where(odd, turned, packed).astype(jnp.bfloat16)
            sides_full[zs, 2 * t + 1] = jnp.where(odd, packed, turned).astype(jnp.bfloat16)
    for a in range(2):
        @pl.when(present[a])
        def passed(a=a):
            pass_copy(a).wait_recv()

    arrived(pivot.at[1 - c], core_recv)

    eye = lax.broadcasted_iota(jnp.int32, (BAND, TILE), 0) == lax.broadcasted_iota(jnp.int32, (BAND, TILE), 1)

    def inverse_of(h):
        found = []
        for t in range(HALF // TILE):
            block = pivot[h, h * (ZS // 2) + t, :, :, t * TILE:(t + 1) * TILE].reshape(BAND, TILE)
            found.append(jnp.sum(jnp.where(eye, block.astype(jnp.float32), 0.0), axis=0, keepdims=True))
        return 1.0 / jnp.concatenate(found, axis=1)

    inverse = [inverse_of(h) for h in range(CORES)]
    def target(a, h):
        block = stacked[a, h].reshape(BAND, HALF).astype(jnp.float32)
        return jnp.where(present[a], block, 0.0)

    for a in range(2):
        for h in range(CORES):
            iterate[0, a * BAND:(a + 1) * BAND, h * HALF:(h + 1) * HALF] = (target(a, h) * inverse[h]).astype(jnp.bfloat16)
    for sweep in range(SWEEPS):
        now, later = sweep % 2, (sweep + 1) % 2
        for h in range(CORES):
            columns = slice(h * HALF, (h + 1) * HALF)
            for a in range(2):
                rows = slice(a * BAND, (a + 1) * BAND)
                moved = jnp.dot(iterate[now, rows], pivot[h].reshape(ZS * BAND, HALF), preferred_element_type=jnp.float32)
                step = (target(a, h) - moved) * inverse[h]
                iterate[later, rows, columns] = (iterate[now, rows, columns].astype(jnp.float32) + step).astype(jnp.bfloat16)

    factor = iterate[SWEEPS % 2]
    coupled = jnp.dot(factor, hand[:, :BAND, :].reshape(ZS * BAND, 2 * TILE), preferred_element_type=jnp.float32)
    upper_part = jnp.where(present[0], coupled[:, :TILE], 0.0).astype(jnp.bfloat16)
    lower_part = jnp.where(present[1], coupled[:, TILE:], 0.0).astype(jnp.bfloat16)
    sides_part = jnp.dot(factor, sides_full[...].reshape(ZS * BAND, TILE), preferred_element_type=jnp.float32).astype(jnp.bfloat16)
    for a in range(2):
        rows = slice(a * BAND, (a + 1) * BAND)
        update[0, a, :, :, 0:TILE] = upper_part[rows].reshape(YS, ROWS, TILE)
        update[0, a, :, :, TILE:2 * TILE] = lower_part[rows].reshape(YS, ROWS, TILE)
        update[0, a, :, :, 2 * TILE:] = sides_part[rows].reshape(YS, ROWS, TILE)

    def back_copy(a, dy):
        to = lax.rem(y + dy, YS)
        return remote(update.at[0, a, to], update.at[1, a, y], back_send.at[a], back_recv.at[a], at(dx=1 if a == 0 else 3, dy=dy))

    for a in range(2):
        @pl.when(present[a])
        def back_start(a=a):
            for dy in (2, 1, 3, 0):
                back_copy(a, dy).start()

    for a in range(2):
        @pl.when(present[1 - a])
        def back_arrival(a=a):
            arrived(update.at[1, a], back_recv.at[a])

    for t in range(YS):
        columns = slice(t * TILE, (t + 1) * TILE)
        before, after = update[1, 0, t].astype(jnp.float32), update[1, 1, t].astype(jnp.float32)
        reduced = pivot_own[:, columns].astype(jnp.float32) - before[:, :TILE] - after[:, TILE:2 * TILE]
        pivot_out[:, columns] = reduced.astype(jnp.bfloat16)
        lower_out[:, columns] = (-before[:, TILE:2 * TILE]).astype(jnp.bfloat16)
        upper_out[:, columns] = (-after[:, :TILE]).astype(jnp.bfloat16)
    for t in range(2):
        columns = slice(t * TILE, (t + 1) * TILE)
        terms = [
            jnp.where(left, update[1, a, 2 * t, :, 2 * TILE:].astype(jnp.float32), update[1, a, 2 * t + 1, :, 2 * TILE:].astype(jnp.float32))
            for a in range(2)
        ]
        reduced = sides_own[:, columns].astype(jnp.float32) - terms[0] - terms[1]
        sides_out[:, columns] = reduced.astype(jnp.bfloat16)

    sent(pivot.at[c, pl.ds(0, ZS - 1), 0], z_send)
    sent(pivot.at[c, pl.ds(0, 6)], y_send)
    sent(pivot.at[c], core_send)
    for a in range(2):
        @pl.when(present[1 - a])
        def stack_sent(a=a):
            sent(stacked.at[a, c], stack_send.at[a])

        @pl.when(present[a])
        def rest_sent(a=a):
            pass_copy(a).wait_send()
            sent(update.at[0, a], back_send.at[a])

    for kind in range(3):
        sent(sides_raw.at[pl.ds(0, YS - 1)], deal_send.at[kind])
    sent(hand.at[pl.ds(0, ZS - 1)], band_send)


def hand_out(*refs):
    sources, results, sem = refs[:4], refs[4:8], refs[8]
    copies = [pltpu.make_async_copy(src, dst, sem.at[i]) for i, (src, dst) in enumerate(zip(sources, results))]
    for copy in copies:
        copy.start()
    for copy in copies:
        copy.wait()


def per_device(diagonals, lower, upper, sides):
    square = jax.ShapeDtypeStruct((ROWS, HALF), jnp.bfloat16)
    wide = jax.ShapeDtypeStruct((ROWS, HALF // 2), jnp.bfloat16)
    whole = pl.BlockSpec(memory_space=pltpu.VMEM)
    bf16 = jnp.bfloat16
    dma = pltpu.SemaphoreType.DMA
    outs = pl.pallas_call(
        kernel,
        out_shape=(square, square, square, wide),
        in_specs=[pl.BlockSpec(memory_space=pltpu.HBM)] * 4,
        out_specs=(whole,) * 4,
        scratch_shapes=[
            pltpu.VMEM((ROWS, HALF), bf16),
            pltpu.VMEM((ROWS, HALF), bf16),
            pltpu.VMEM((ROWS, HALF), bf16),
            pltpu.VMEM((ROWS, HALF // 2), bf16),
            pltpu.VMEM((CORES, ZS, YS, ROWS, HALF), bf16),
            pltpu.VMEM((2, CORES, YS, ROWS, HALF), bf16),
            pltpu.VMEM((YS, ROWS, TILE), bf16),
            pltpu.VMEM((ZS, PACKED, 2 * TILE), bf16),
            pltpu.VMEM((ZS, YS, ROWS, TILE), bf16),
            pltpu.VMEM((2, 2 * BAND, CORES * HALF), bf16),
            pltpu.VMEM((2 * BAND, HALF), jnp.float32),
            pltpu.VMEM((2, 2, YS, ROWS, 3 * TILE), bf16),
            dma((8,)),
            dma, dma((ZS,)),
            dma, dma((ZS,)),
            dma, dma,
            dma((2,)), dma((2,)),
            dma((2,)), dma((2,)),
            dma((3,)), dma((3,)),
            dma, dma((ZS,)),
            dma((2,)), dma((2,)),
        ],
        compiler_params=pltpu.CompilerParams(
            collective_id=0, has_side_effects=True, vmem_limit_bytes=55104 * 2**10
        ),
    )(*(pltpu.with_memory_space_constraint(array[0], pltpu.HBM) for array in (diagonals, lower, upper, sides)))
    outs = pl.pallas_call(
        hand_out,
        out_shape=(square, square, square, wide),
        in_specs=[pl.BlockSpec(memory_space=pl.ANY)] * 4,
        out_specs=[pl.BlockSpec(memory_space=pl.ANY)] * 4,
        scratch_shapes=[dma((4,))],
        compiler_params=pltpu.CompilerParams(vmem_limit_bytes=55104 * 2**10),
    )(*outs)
    return tuple(out[None] for out in outs)


def solution(mesh):
    spec = P("slab", "row", "col")
    return jax.shard_map(
        per_device, mesh=mesh, in_specs=(spec,) * 4, out_specs=(spec,) * 4, check_vma=False
    )
```
